32 devices in a mesh: gx: 8 (over z, y), gy: 4 (over x, core).
Axes of the slice: x: 2, y: 2, z: 4, core: 2. Of those that a mesh axis runs over, the one named last changes fastest.
Arguments:
- fields: float32 [4, 8, 1024, 512], P(None, None, 'gx', 'gy'), may hold values from -6 to 6
- shift_x: float32 [8, 1024, 512], P(None, 'gx', 'gy'), may hold values from -0.5 to 0.5
- shift_y: float32 [8, 1024, 512], P(None, 'gx', 'gy'), may hold values from -0.5 to 0.5
- block_offset: int32 [64, 4], P(None, 'gy'), may hold values from -23 to 23, as said below
- group_inverse: float32 [8, 1024, 128], P(None, 'gx'), as said below
- lower_coupling: float32 [8, 8], P(None, 'gx'), as said below
- upper_coupling: float32 [8, 8], P(None, 'gx'), as said below
Outputs:
- wind_fields: float32 [2, 8, 1024, 512], P(None, None, 'gx', 'gy')
- tracers: float32 [2, 8, 1024, 512], P(None, None, 'gx', 'gy')
The draws below stay inside these ranges and needn't reach their ends.
Inputs may be any that keep to these rules, and one draw needn't show every extreme that they name: `block_offset`: within each aligned run of 8 x-blocks (the blocks of 128 consecutive columns at one y-block), every block departs from a block in the same run or in one of the two runs before or after it, and that run lies inside the grid; at most 4 blocks of a run depart from any one run, and exactly 4 depart from a run two runs away. `group_inverse`: entries are positive. `lower_coupling`: Negative. `upper_coupling`: Negative.
All inputs are finite; a program needn't handle non-finite values.
Results may differ from the reference program's by a relative error of at most 0.0003.
Values sent between devices are 32-bit elements; how exact they have to be, the bound alone decides.
A program may use at most 128 MiB of HBM per device.

```python
import math
import jax
import jax.numpy as jnp
from jax import lax

FIELDS = 4
MODEL_LEVELS = 8
CX = 128
CY = 128
BX = 16
NBX = 8
CAP = 4
NX = 1024
NY = 512
NXB = 64
PADX = 258
N_GX = 8
N_GY = 4


def draw_block_offset(key, part):
    root_random_key = jax.random.fold_in(key, 3)
    score_key = jax.random.fold_in(root_random_key, 1)
    pick_key = jax.random.fold_in(root_random_key, 2)
    local_key = jax.random.fold_in(root_random_key, 3)
    group_place = jnp.arange(N_GX, dtype=jnp.int32)[:, None, None]
    row_place = jnp.arange(N_GY, dtype=jnp.int32)[None, None, :]
    parity_side = jnp.where((group_place + row_place) % 2 == 1, -2, 2)
    primary = jnp.where(group_place < 2, 2, jnp.where(group_place >= N_GX - 2, -2, parity_side))
    inside = jnp.arange(NBX, dtype=jnp.int32)[None, :, None]
    scores = jax.random.randint(score_key, (N_GX, NBX, N_GY), 0, 1 << 20) * NBX + inside
    ranking = jnp.argsort(jnp.argsort(scores, axis=1), axis=1)
    picked = jax.random.randint(pick_key, (N_GX, NBX, N_GY), 0, 4)
    others = picked - 2 + jnp.where(primary == -2, 1, 0)
    others = jnp.clip(others, -group_place, N_GX - 1 - group_place)
    distance = jnp.where(ranking < CAP, primary, others)
    source_random = jax.random.randint(local_key, (N_GX, NBX, N_GY), 0, NBX)
    edge_source = jnp.where(primary == -2, 0, NBX - 1)
    source_local = jnp.where(ranking == 0, edge_source, source_random)
    offsets = inside - source_local - distance * NBX
    return offsets.reshape(NXB, N_GY).astype(jnp.int32)


def interface_draw(key):
    root_random_key = jax.random.fold_in(key, 4)
    coarse_random_key, diagonal_random_key, category_random_key, gentle_random_key, quick_random_key, surge_random_key, level_depth_key = jax.random.split(root_random_key, 7)
    rows_in = (jnp.arange(NX, dtype=jnp.int32) % CX)[:, None]
    cols_in = jnp.arange(CX, dtype=jnp.int32)[None, :]
    spacing = jnp.abs(rows_in - cols_in).astype(jnp.float32)
    smooth = jnp.exp(-spacing / (2.0 * CX))
    rough = jax.random.uniform(coarse_random_key, (MODEL_LEVELS, NX, CX), jnp.float32, -1.0, 1.0)
    diagonal = jax.random.uniform(diagonal_random_key, (MODEL_LEVELS, NX, 1), jnp.float32, 0.3, 0.9)
    on_diagonal = jnp.where(rows_in == cols_in, 1.0, 0.0).astype(jnp.float32)
    entries = smooth[None] * (1.0 + 0.3 * rough) + on_diagonal[None] * diagonal
    rows_float = rows_in.astype(jnp.float32)
    ramp_first = jnp.exp(-3.9 * (CX - 1.0 - rows_float) / (CX - 1.0))
    ramp_last = jnp.exp(-3.9 * rows_float / (CX - 1.0))
    first_column = ramp_first[None] * (1.0 + 0.3 * rough[:, :, 0:1])
    last_column = ramp_last[None] * (1.0 + 0.3 * rough[:, :, CX - 1:CX])
    entries = jnp.where(cols_in[None] == 0, first_column, jnp.where(cols_in[None] == CX - 1, last_column, entries))
    inverse = entries / math.sqrt(CX)
    blocks = inverse.reshape(MODEL_LEVELS, N_GX, CX, CX)
    far_first = blocks[:, :, CX - 1, 0]
    far_last = blocks[:, :, 0, CX - 1]
    level_rank = jax.random.permutation(category_random_key, MODEL_LEVELS)
    slow_count = max(1, MODEL_LEVELS // 2)
    gentle_level = (level_rank < slow_count)[None, :, None]
    slow_rate = min(math.exp(math.log(0.2) / N_GX), 0.95)
    gentle_rate_values = slow_rate * jax.random.uniform(gentle_random_key, (2, MODEL_LEVELS, N_GX), jnp.float32, 0.985, 1.0)
    quick_rate_values = jax.random.uniform(quick_random_key, (2, MODEL_LEVELS, N_GX), jnp.float32, 0.57, 0.6)
    surge_level_draw = jax.random.uniform(surge_random_key, (2, MODEL_LEVELS, N_GX), jnp.float32, 0.0, 1.0)
    surge_level_depth = jax.random.uniform(level_depth_key, (2, MODEL_LEVELS, N_GX), jnp.float32, 0.5, 0.8)
    level_rates = jnp.where(gentle_level, gentle_rate_values, quick_rate_values) * jnp.where(surge_level_draw < 0.1, surge_level_depth, 1.0)
    lower = -level_rates[0] / far_first
    upper = -level_rates[1] / far_last
    return (inverse, lower, upper)


def draw_group_inverse(key, part):
    return interface_draw(key)[0]


def draw_lower_coupling(key, part):
    return interface_draw(key)[1]


def draw_upper_coupling(key, part):
    return interface_draw(key)[2]


def levels(stream_key, dims, shards, low, largest):
    gain = 1.0
    for axis_at, shards_of in shards:
        draws = jax.random.uniform(jax.random.fold_in(jax.random.fold_in(stream_key, 6), axis_at), (shards_of,), jnp.float32, low / len(shards), largest / len(shards))
        gain = gain * jnp.repeat(jnp.exp(draws), dims[axis_at] // shards_of).reshape((-1,) + (1,) * (len(dims) - 1 - axis_at))
    return gain


def scatter_about(key, dims, width, bound, cuts=(), kind=jnp.bfloat16):
    drawn = jax.random.normal(key, dims, jnp.float32) * width
    if len(cuts) > 0:
        drawn = levels(key, dims, cuts, -0.22, 0.18) * drawn
    return jnp.clip(drawn, min=-bound, max=bound).astype(kind)


def setup_inputs(seed: int = 0) -> dict:
    arg_keys = jax.random.split(jax.random.key(seed), 8)
    return {
        "fields": scatter_about(arg_keys[0], (FIELDS, MODEL_LEVELS, NX, NY), 1.0, 6.0, ((2, 8), (3, 4)), jnp.float32),
        "shift_x": jnp.clip(jax.random.uniform(arg_keys[1], (MODEL_LEVELS, NX, NY), jnp.float32, -0.5, 0.5) * levels(arg_keys[1], (MODEL_LEVELS, NX, NY), ((1, 8), (2, 4)), -0.4, 0.0), -0.5, 0.5),
        "shift_y": jnp.clip(jax.random.uniform(arg_keys[2], (MODEL_LEVELS, NX, NY), jnp.float32, -0.5, 0.5) * levels(arg_keys[2], (MODEL_LEVELS, NX, NY), ((1, 8), (2, 4)), -0.4, 0.0), -0.5, 0.5),
        "block_offset": draw_block_offset(jax.random.fold_in(arg_keys[7], 71), 0),
        "group_inverse": draw_group_inverse(jax.random.fold_in(arg_keys[7], 71), 0),
        "lower_coupling": draw_lower_coupling(jax.random.fold_in(arg_keys[7], 71), 0),
        "upper_coupling": draw_upper_coupling(jax.random.fold_in(arg_keys[7], 71), 0),
    }


PRECISE = lax.Precision.HIGHEST

def lagrange(displace):
    position = -displace
    weights = []
    for target in range(-2, 3):
        factor = jnp.ones_like(position)
        for anchor in range(-2, 3):
            if anchor != target:
                factor = factor * ((position - anchor) / (target - anchor))
        weights.append(factor)
    return weights

def interpolate(window, across, along, span_x, span_y):
    weights_x = lagrange(across)
    weights_y = lagrange(along)
    running_total = None
    for column_tap in range(5):
        partial_sum = weights_y[0] * window[..., column_tap:column_tap + span_x, 0:span_y]
        for row_tap in range(1, 5):
            partial_sum = partial_sum + weights_y[row_tap] * window[..., column_tap:column_tap + span_x, row_tap:row_tap + span_y]
        tap_term = weights_x[column_tap] * partial_sum
        running_total = tap_term if running_total is None else running_total + tap_term
    return running_total

def advect(fields, shift_x, shift_y, block_offset):
    padded = jnp.pad(fields, ((0, 0), (0, 0), (PADX, PADX), (2, 2)))
    blocks_x = NX // BX
    blocks_y = N_GY

    def one_block(flat_index):
        column_block = flat_index // blocks_y
        row_block = flat_index % blocks_y
        offset_here = block_offset[column_block, row_block].astype(jnp.int32)
        start_x = ((column_block - offset_here) * BX + PADX - 2).astype(jnp.int32)
        start_y = (row_block * CY).astype(jnp.int32)
        zero_index = jnp.zeros((), jnp.int32)
        window = lax.dynamic_slice(padded, (zero_index, zero_index, start_x, start_y), (FIELDS, MODEL_LEVELS, BX + 4, CY + 4))
        root_x = (column_block * BX).astype(jnp.int32)
        across = lax.dynamic_slice(shift_x, (zero_index, root_x, start_y), (MODEL_LEVELS, BX, CY))
        along = lax.dynamic_slice(shift_y, (zero_index, root_x, start_y), (MODEL_LEVELS, BX, CY))
        return interpolate(window, across[None], along[None], BX, CY)
    gathered = lax.map(one_block, jnp.arange(blocks_x * blocks_y, dtype=jnp.int32))
    gathered = gathered.reshape(blocks_x, blocks_y, FIELDS, MODEL_LEVELS, BX, CY)
    return gathered.transpose(2, 3, 0, 4, 1, 5).reshape(FIELDS, MODEL_LEVELS, NX, NY)

def implicit_sweep(winds_in, group_inverse, lower_coupling, upper_coupling):
    chains = N_GX
    inverse = group_inverse.reshape(MODEL_LEVELS, chains, CX, CX)
    right_side = winds_in.reshape(2, MODEL_LEVELS, chains, CX, NY)
    local_solve = jnp.einsum('ldij,wldjy->wldiy', inverse, right_side, precision=PRECISE)
    first_row = local_solve[:, :, :, 0, :]
    last_row = local_solve[:, :, :, CX - 1, :]
    left_spike = inverse[:, :, :, 0] * lower_coupling[:, :, None]
    right_spike = inverse[:, :, :, CX - 1] * upper_coupling[:, :, None]
    lead_left = left_spike[:, :, 0]
    tail_left = left_spike[:, :, CX - 1]
    lead_right = right_spike[:, :, 0]
    tail_right = right_spike[:, :, CX - 1]
    unknowns = 2 * chains
    matrix = jnp.broadcast_to(jnp.eye(unknowns, dtype=jnp.float32), (MODEL_LEVELS, unknowns, unknowns))
    chain_index = jnp.arange(chains, dtype=jnp.int32)
    later_chain = chain_index[1:]
    early_chain = chain_index[:-1]
    matrix = matrix.at[:, 2 * later_chain, 2 * later_chain - 1].set(lead_left[:, 1:])
    matrix = matrix.at[:, 2 * early_chain, 2 * early_chain + 2].set(lead_right[:, :-1])
    matrix = matrix.at[:, 2 * later_chain + 1, 2 * later_chain - 1].set(tail_left[:, 1:])
    matrix = matrix.at[:, 2 * early_chain + 1, 2 * early_chain + 2].set(tail_right[:, :-1])
    reduced_side = jnp.stack([first_row, last_row], axis=3)
    reduced_side = reduced_side.transpose(1, 2, 3, 0, 4).reshape(MODEL_LEVELS, unknowns, 2 * NY)
    solved = jnp.linalg.solve(matrix, reduced_side).reshape(MODEL_LEVELS, chains, 2, 2, NY)
    first_all = solved[:, :, 0].transpose(2, 0, 1, 3)
    last_all = solved[:, :, 1].transpose(2, 0, 1, 3)
    zero_chain = jnp.zeros_like(first_all[:, :, :1])
    left_value = jnp.concatenate([zero_chain, last_all[:, :, :-1]], axis=2)
    right_value = jnp.concatenate([first_all[:, :, 1:], zero_chain], axis=2)
    wind_fields = local_solve - left_spike[None, :, :, :, None] * left_value[:, :, :, None, :] - right_spike[None, :, :, :, None] * right_value[:, :, :, None, :]
    return wind_fields.reshape(2, MODEL_LEVELS, NX, NY)

def reference(fields, shift_x, shift_y, block_offset, group_inverse, lower_coupling, upper_coupling):
    advected = advect(fields, shift_x, shift_y, block_offset)
    wind_fields = implicit_sweep(advected[0:2], group_inverse, lower_coupling, upper_coupling)
    return (wind_fields, advected[2:4])
```

```python
import functools

import jax
import jax.numpy as jnp
from jax import lax
from jax.experimental import pallas as pl
from jax.experimental.pallas import tpu as pltpu
from jax.sharding import PartitionSpec as P

BX = 16
CAP = 4
DELTA = (2, -2, 1, -1)
REMOTE = CAP * len(DELTA)
SLOTS = REMOTE + CAP
ROWS = BX + 5
MESH = pl.DeviceIdType.MESH


def weights_of(shift):
    p = -shift
    a, b, c, d = p + 2.0, p + 1.0, p - 1.0, p - 2.0
    ab, cd = a * b, c * d
    pcd, pab = p * cd, p * ab
    return (
        b * pcd * (1.0 / 24.0),
        a * pcd * (-1.0 / 6.0),
        ab * cd * 0.25,
        pab * d * (-1.0 / 6.0),
        pab * c * (1.0 / 24.0),
    )


def kernel(
    n, m, nb,
    offs, xm, shx, shy, ginv, low, upp,
    wind, tracers,
    side_rows, edge, edge_lo, edge_hi, rims, send, recv, adv, wgt, solved, spikes, coef, iface, work,
    ilist, blist,
    halo_s, halo_r, slot_s, slot_r, rim_s, rim_r, coef_s, coef_r, if_s, if_r,
):
    levels, cols, lanes = 8, nb * BX, 128
    s, r = lax.axis_index("gx"), lax.axis_index("gy")
    lane = lax.broadcasted_iota(jnp.int32, (8, lanes), 1)
    zero = jnp.zeros((8, lanes), jnp.float32)

    def valid(ds, dr):
        return (s + ds >= 0) & (s + ds < n) & (r + dr >= 0) & (r + dr < m)

    for f in range(4):
        for x in range(4):
            side_rows[x, f] = zero
        for b in range(nb + 2):
            edge_lo[b, f] = zero
            edge_hi[b, f] = zero

    barrier = pltpu.get_barrier_semaphore()
    diagonal = [(ds, dr) for ds in (-1, 0, 1) for dr in (-1, 1)]

    def greet(d, carry):
        @pl.when(d != s)
        def _():
            pl.semaphore_signal(barrier, inc=1, device_id=(d, r), device_id_type=MESH)
        return carry

    lax.fori_loop(0, n, greet, 0)
    for ds, dr in diagonal:
        @pl.when(valid(ds, dr))
        def _():
            pl.semaphore_signal(barrier, inc=1, device_id=(s + ds, r + dr), device_id_type=MESH)

    def edges(b, carry):
        for f in range(4):
            acc = zero
            for j in range(BX):
                at = 4 * (j + 2)
                moved = pltpu.roll(xm[b * BX + j, f], at, 1)
                acc = jnp.where((lane >= at - 2) & (lane < at + 2), moved, acc)
            edge[b, f] = acc
        return carry

    lax.fori_loop(0, nb, edges, 0)

    lower = jnp.broadcast_to(low[...], (8, lanes))
    upper = jnp.broadcast_to(upp[...], (8, lanes))
    first = jnp.concatenate([ginv[l * cols:l * cols + 1, :] for l in range(levels)], axis=0)
    final = jnp.concatenate([ginv[(l + 1) * cols - 1:(l + 1) * cols, :] for l in range(levels)], axis=0)
    coef[s, 0] = jnp.broadcast_to(first[:, 0:1], (8, lanes)) * lower
    coef[s, 1] = jnp.broadcast_to(final[:, 0:1], (8, lanes)) * lower
    coef[s, 2] = jnp.broadcast_to(first[:, cols - 1:cols], (8, lanes)) * upper
    coef[s, 3] = jnp.broadcast_to(final[:, cols - 1:cols], (8, lanes)) * upper

    def listed(dest, source):
        base = jnp.clip(dest, 0, n - 1) * nb
        count = jnp.int32(0)
        picks = [(jnp.int32(0), jnp.int32(0)) for _ in range(CAP)]
        for i in range(nb):
            g = base + i - offs[base + i]
            hit = (g >= source * nb) & (g < source * nb + nb)
            for k in range(CAP):
                here = hit & (count == k)
                picks[k] = (
                    jnp.where(here, jnp.int32(i), picks[k][0]),
                    jnp.where(here, g - source * nb, picks[k][1]),
                )
            count = count + jnp.where(hit, 1, 0)
        return picks

    for e, delta in enumerate(DELTA):
        outgoing = listed(s + delta, s)
        incoming = listed(s, s - delta)
        for k in range(CAP):
            blist[k * 4 + e] = outgoing[k][1]
            ilist[k * 4 + e] = incoming[k][0]
    own = listed(s, s)
    for k in range(CAP):
        blist[REMOTE + k] = own[k][1]
        ilist[REMOTE + k] = own[k][0]

    pl.semaphore_wait(
        barrier, n - 1 + sum(jnp.where(valid(ds, dr), 1, 0) for ds, dr in diagonal)
    )

    halo = [
        (1, 0, xm.at[pl.ds(cols - 2, 2)], side_rows.at[pl.ds(0, 2)]),
        (-1, 0, xm.at[pl.ds(0, 2)], side_rows.at[pl.ds(2, 2)]),
        (0, 1, edge, edge_lo.at[pl.ds(1, nb)]),
        (0, -1, edge, edge_hi.at[pl.ds(1, nb)]),
        (1, 1, edge.at[nb - 1], edge_lo.at[0]),
        (1, -1, edge.at[nb - 1], edge_hi.at[0]),
        (-1, 1, edge.at[0], edge_lo.at[nb + 1]),
        (-1, -1, edge.at[0], edge_hi.at[nb + 1]),
    ]

    def halo_copy(q):
        ds, dr, source, target = halo[q]
        return pltpu.make_async_remote_copy(
            src_ref=source, dst_ref=target, send_sem=halo_s.at[q], recv_sem=halo_r.at[q],
            device_id=(s + ds, r + dr), device_id_type=MESH,
        )

    for q in range(8):
        @pl.when(valid(halo[q][0], halo[q][1]))
        def _(q=q):
            halo_copy(q).start()

    def share(buffer, sends, recvs, d):
        return pltpu.make_async_remote_copy(
            src_ref=buffer.at[s], dst_ref=buffer.at[s], send_sem=sends.at[d],
            recv_sem=recvs.at[s], device_id=(d, r), device_id_type=MESH,
        )

    def shared(buffer, sends, recvs, d):
        return pltpu.make_async_remote_copy(
            src_ref=buffer.at[d], dst_ref=buffer.at[d], send_sem=sends.at[d],
            recv_sem=recvs.at[d], device_id=(d, r), device_id_type=MESH,
        )

    def others(act):
        def step(d, carry):
            @pl.when(d != s)
            def _():
                act(d)
            return carry
        lax.fori_loop(0, n, step, 0)

    def part_copy(slot, e, lo, size, sends, recvs, index):
        return pltpu.make_async_remote_copy(
            src_ref=send.at[slot, pl.ds(lo, size)], dst_ref=recv.at[slot, pl.ds(lo, size)],
            send_sem=sends.at[index], recv_sem=recvs.at[index],
            device_id=(s + DELTA[e], r), device_id_type=MESH,
        )

    def centre(into, slot, b):
        def row(j, carry):
            for f in range(4):
                into[slot, j, f] = xm[b * BX + j, f]
            return carry
        lax.fori_loop(0, BX, row, 0, unroll=4)

    def rim(into, slot, b):
        for j in range(5):
            for f in range(4):
                into[slot, BX + j, f] = rims[b, j, f]

    for e, delta in enumerate(DELTA):
        @pl.when(valid(delta, 0))
        def _(e=e):
            centre(send, e, blist[e])
            part_copy(e, e, 0, BX, slot_s, slot_r, e).start()

    others(lambda d: share(coef, coef_s, coef_r, d).start())

    for q in range(8):
        @pl.when(valid(-halo[q][0], -halo[q][1]))
        def _(q=q):
            halo_copy(q).wait_recv()

    before = ((lane + 2) & 3) < 2

    def make_rims(b, carry):
        for f in range(4):
            mid = jnp.where(before, edge_lo[b + 1, f], edge_hi[b + 1, f])
            prev = jnp.where(before, edge_lo[b, f], edge_hi[b, f])
            after = jnp.where(before, edge_lo[b + 2, f], edge_hi[b + 2, f])
            mid = jnp.where((lane >= 126) | (lane < 6), pltpu.roll(prev, 64, 1), mid)
            rims[b, 4, f] = jnp.where((lane >= 70) & (lane < 78), pltpu.roll(after, 64, 1), mid)
        return carry

    lax.fori_loop(0, nb, make_rims, 0)

    for b in range(nb):
        for f in range(4):
            for j in range(2):
                rims[b, j, f] = xm[b * BX - 2 + j, f] if b else side_rows[j, f]
                rims[b, 2 + j, f] = xm[b * BX + BX + j, f] if b < nb - 1 else side_rows[2 + j, f]

    for e, delta in enumerate(DELTA):
        @pl.when(valid(delta, 0))
        def _(e=e):
            rim(send, e, blist[e])
            part_copy(e, e, BX, 5, rim_s, rim_r, e).start()

    for k in range(1, CAP):
        for e, delta in enumerate(DELTA):
            @pl.when(valid(delta, 0))
            def _(e=e, slot=k * 4 + e):
                centre(send, slot, blist[slot])
                rim(send, slot, blist[slot])
                part_copy(slot, e, 0, ROWS, slot_s, slot_r, slot).start()

    for l in range(levels):
        def spike(x, carry, l=l):
            g = ginv[pl.ds(l * cols + x * 8, 8), :]
            spikes[0, l, pl.ds(x * 8, 8), :] = (
                jnp.broadcast_to(g[:, 0:1], (8, lanes)) * jnp.broadcast_to(low[l:l + 1, :], (8, lanes))
            )
            spikes[1, l, pl.ds(x * 8, 8), :] = (
                jnp.broadcast_to(g[:, cols - 1:cols], (8, lanes))
                * jnp.broadcast_to(upp[l:l + 1, :], (8, lanes))
            )
            return carry
        lax.fori_loop(0, cols // 8, spike, 0)

    def advect(buffer, slot):
        i = ilist[slot]

        def weigh(j, carry):
            for q, w in enumerate(weights_of(shx[i * BX + j])):
                wgt[j, q] = w
            for q, w in enumerate(weights_of(shy[i * BX + j])):
                wgt[j, 5 + q] = w
            return carry

        lax.fori_loop(0, BX, weigh, 0, unroll=2)

        def field(f, carry):
            side = buffer[slot, BX + 4, f]
            rows = []
            for x in range(BX + 4):
                at = BX + x if x < 2 else (x - 2 if x < BX + 2 else x)
                mid = buffer[slot, at, f]
                rimmed = side if x == 0 else pltpu.roll(side, lanes - 4 * x, 1)
                rows.append((
                    pltpu.roll(jnp.where(lane >= 126, rimmed, mid), 2, 1),
                    pltpu.roll(jnp.where(lane >= 127, rimmed, mid), 1, 1),
                    mid,
                    pltpu.roll(jnp.where(lane < 1, rimmed, mid), lanes - 1, 1),
                    pltpu.roll(jnp.where(lane < 2, rimmed, mid), lanes - 2, 1),
                ))
                if x >= 4:
                    j = x - 4
                    wy = [wgt[j, 5 + q] for q in range(5)]
                    total = None
                    for a in range(5):
                        part = wy[0] * rows[j + a][0]
                        for q in range(1, 5):
                            part = part + wy[q] * rows[j + a][q]
                        part = wgt[j, a] * part
                        total = part if total is None else total + part
                    adv[slot, pl.ds(f * levels * BX + j, levels, stride=BX), :] = total
            return carry

        lax.fori_loop(0, 4, field, 0)

    def local_slot(k, carry):
        slot = REMOTE + k
        b = blist[slot]
        centre(recv, slot, b)
        rim(recv, slot, b)
        advect(recv, slot)
        return carry

    lax.fori_loop(0, CAP, local_slot, 0)

    others(lambda d: shared(coef, coef_s, coef_r, d).wait_recv())

    def pivot_step(d, gain):
        ll, tl, lr, tr = (coef[d, q] for q in range(4))
        inverse = 1.0 / (1.0 - ll * gain)
        ratio = tl * gain * inverse
        work[d, 0] = gain
        work[d, 1] = inverse
        work[d, 2] = ratio
        return tr + ratio * lr

    lax.fori_loop(0, n, pivot_step, zero)

    for k in range(CAP):
        for e, delta in enumerate(DELTA):
            @pl.when(valid(-delta, 0))
            def _(e=e, k=k, slot=k * 4 + e):
                if k == 0:
                    part_copy(slot, e, 0, BX, slot_s, slot_r, slot).wait_recv()
                    part_copy(slot, e, BX, 5, rim_s, rim_r, e).wait_recv()
                else:
                    part_copy(slot, e, 0, ROWS, slot_s, slot_r, slot).wait_recv()
        def remote_slot(e, carry, k=k):
            advect(recv, k * 4 + e)
            return carry
        lax.fori_loop(0, 4, remote_slot, 0)

    runs = []
    for i in range(nb):
        g = s * nb + i - offs[s * nb + i]
        runs.append(lax.shift_right_arithmetic(g, jnp.int32(nb.bit_length() - 1)))
    for i in range(nb):
        count = jnp.int32(0)
        for j in range(i):
            count = count + jnp.where(runs[j] == runs[i], 1, 0)
        count = jnp.minimum(count, CAP - 1)
        gap = s - runs[i]
        place = REMOTE + count
        for e, delta in enumerate(DELTA):
            place = jnp.where(gap == delta, count * 4 + e, place)

        def put(l, carry, i=i, place=place):
            for w in range(2):
                at = pl.multiple_of((w * levels + l) * BX, BX)
                solved[w, l, pl.ds(i * BX, BX), :] = adv[place, pl.ds(at, BX), :]
                at = pl.multiple_of(((w + 2) * levels + l) * BX, BX)
                tracers[w, l, pl.ds(i * BX, BX), :] = adv[place, pl.ds(at, BX), :]
            return carry

        lax.fori_loop(0, levels, put, 0)

    def solve(l, carry):
        right = jnp.concatenate([solved[0, l], solved[1, l]], axis=1)
        g = ginv[pl.ds(pl.multiple_of(l * cols, cols), cols), :]
        out = jnp.dot(g, right, precision=lax.Precision.HIGHEST, preferred_element_type=jnp.float32)
        for w in range(2):
            part = out[:, w * lanes:(w + 1) * lanes]
            solved[w, l] = part
            iface[s, w, pl.ds(l, 1), :] = part[0:1]
            iface[s, 2 + w, pl.ds(l, 1), :] = part[cols - 1:cols]
        return carry

    lax.fori_loop(0, levels, solve, 0)

    others(lambda d: share(iface, if_s, if_r, d).start())
    others(lambda d: shared(iface, if_s, if_r, d).wait_recv())

    def forward(d, behind):
        ll, tl, ratio = coef[d, 0], coef[d, 1], work[d, 2]
        after = []
        for w in range(2):
            lead = iface[d, w] - ll * behind[w]
            work[d, 3 + w] = lead
            work[d, 5 + w] = behind[w]
            after.append(iface[d, 2 + w] - tl * behind[w] + ratio * lead)
        return tuple(after)

    lax.fori_loop(0, n, forward, (zero, zero))

    def backward(k, ahead):
        d = n - 1 - k
        lr, inverse = coef[d, 2], work[d, 1]
        values = []
        for w in range(2):
            work[d, 7 + w] = ahead[w]
            values.append((work[d, 3 + w] - lr * ahead[w]) * inverse)
            work[d, 9 + w] = values[w]
        return tuple(values)

    lax.fori_loop(0, n - s, backward, (zero, zero))

    for w in range(2):
        left = work[s, 5 + w] - work[s, 0] * work[s, 9 + w]
        ahead = work[s, 7 + w]
        for l in range(levels):
            here = left[l:l + 1]
            there = ahead[l:l + 1]
            wind[w, l] = solved[w, l] - spikes[0, l] * here - spikes[1, l] * there

    for q in range(8):
        @pl.when(valid(halo[q][0], halo[q][1]))
        def _(q=q):
            halo_copy(q).wait_send()
    others(lambda d: share(coef, coef_s, coef_r, d).wait_send())
    others(lambda d: share(iface, if_s, if_r, d).wait_send())
    for e, delta in enumerate(DELTA):
        @pl.when(valid(delta, 0))
        def _(e=e):
            part_copy(e, e, 0, BX, slot_s, slot_r, e).wait_send()
            part_copy(e, e, BX, 5, rim_s, rim_r, e).wait_send()
            for k in range(1, CAP):
                part_copy(k * 4 + e, e, 0, ROWS, slot_s, slot_r, k * 4 + e).wait_send()


def local(n, m, fields, shift_x, shift_y, block_offset, group_inverse, lower, upper):
    nf, levels, cols, lanes = fields.shape
    nb = cols // BX
    vmem = pl.BlockSpec(memory_space=pltpu.VMEM)
    f32 = jnp.float32
    tile = (8, lanes)
    dma = pltpu.SemaphoreType.DMA
    return pl.pallas_call(
        functools.partial(kernel, n, m, nb),
        out_shape=(
            jax.ShapeDtypeStruct((2, levels, cols, lanes), f32),
            jax.ShapeDtypeStruct((2, levels, cols, lanes), f32),
        ),
        in_specs=[pl.BlockSpec(memory_space=pltpu.SMEM)] + [vmem] * 6,
        out_specs=(vmem, vmem),
        scratch_shapes=[
            pltpu.VMEM((4, nf) + tile, f32),
            pltpu.VMEM((nb, nf) + tile, f32),
            pltpu.VMEM((nb + 2, nf) + tile, f32),
            pltpu.VMEM((nb + 2, nf) + tile, f32),
            pltpu.VMEM((nb, 5, nf) + tile, f32),
            pltpu.VMEM((REMOTE, ROWS, nf) + tile, f32),
            pltpu.VMEM((SLOTS, ROWS, nf) + tile, f32),
            pltpu.VMEM((SLOTS, (nf * levels + 1) * BX, lanes), f32),
            pltpu.VMEM((BX, 10) + tile, f32),
            pltpu.VMEM((2, levels, cols, lanes), f32),
            pltpu.VMEM((2, levels, cols, lanes), f32),
            pltpu.VMEM((n, 4) + tile, f32),
            pltpu.VMEM((n, 4) + tile, f32),
            pltpu.VMEM((n, 11) + tile, f32),
            pltpu.SMEM((SLOTS,), jnp.int32),
            pltpu.SMEM((SLOTS,), jnp.int32),
            dma((8,)), dma((8,)), dma((REMOTE,)), dma((REMOTE,)), dma((4,)), dma((4,)),
            dma((n,)), dma((n,)), dma((n,)), dma((n,)),
        ],
        compiler_params=pltpu.CompilerParams(
            collective_id=0, has_side_effects=True, vmem_limit_bytes=50 * 1024 * 1024
        ),
    )(
        block_offset[:, 0],
        fields.transpose(2, 0, 1, 3),
        shift_x.transpose(1, 0, 2),
        shift_y.transpose(1, 0, 2),
        group_inverse.reshape(-1, cols),
        lower,
        upper,
    )


def solution(mesh):
    return jax.shard_map(
        functools.partial(local, mesh.shape["gx"], mesh.shape["gy"]),
        mesh=mesh,
        in_specs=(
            P(None, None, "gx", "gy"),
            P(None, "gx", "gy"),
            P(None, "gx", "gy"),
            P(None, "gy"),
            P(None, "gx", None),
            P(None, "gx"),
            P(None, "gx"),
        ),
        out_specs=(P(None, None, "gx", "gy"), P(None, None, "gx", "gy")),
        check_vma=False,
    )
```

```python
import functools

import jax
import jax.numpy as jnp
from jax import lax
from jax.experimental import pallas as pl
from jax.experimental.pallas import tpu as pltpu
from jax.sharding import PartitionSpec as P

BX = 16
CAP = 4
DELTA = (2, -2, 1, -1)
REMOTE = CAP * len(DELTA)
SLOTS = REMOTE + CAP
ROWS = BX + 5
MESH = pl.DeviceIdType.MESH


def weights_of(shift):
    p = -shift
    a, b, c, d = p + 2.0, p + 1.0, p - 1.0, p - 2.0
    ab, cd = a * b, c * d
    pcd, pab = p * cd, p * ab
    return (
        b * pcd * (1.0 / 24.0),
        a * pcd * (-1.0 / 6.0),
        ab * cd * 0.25,
        pab * d * (-1.0 / 6.0),
        pab * c * (1.0 / 24.0),
    )


def kernel(
    n, m, nb,
    offs, xm, shx, shy, ginv, low, upp,
    wind, tracers,
    side_rows, edge, edge_lo, edge_hi, rims, send, recv, adv, wgt, solved, spikes, coef, iface, work,
    ilist, blist,
    halo_s, halo_r, slot_s, slot_r, rim_s, rim_r, coef_s, coef_r, if_s, if_r,
):
    levels, cols, lanes = 8, nb * BX, 128
    s, r = lax.axis_index("gx"), lax.axis_index("gy")
    lane = lax.broadcasted_iota(jnp.int32, (8, lanes), 1)
    zero = jnp.zeros((8, lanes), jnp.float32)

    def valid(ds, dr):
        return (s + ds >= 0) & (s + ds < n) & (r + dr >= 0) & (r + dr < m)

    for f in range(4):
        for x in range(4):
            side_rows[x, f] = zero
        for b in range(nb + 2):
            edge_lo[b, f] = zero
            edge_hi[b, f] = zero

    barrier = pltpu.get_barrier_semaphore()
    diagonal = [(ds, dr) for ds in (-1, 0, 1) for dr in (-1, 1)]

    def greet(d, carry):
        @pl.when(d != s)
        def _():
            pl.semaphore_signal(barrier, inc=1, device_id=(d, r), device_id_type=MESH)
        return carry

    lax.fori_loop(0, n, greet, 0)
    for ds, dr in diagonal:
        @pl.when(valid(ds, dr))
        def _():
            pl.semaphore_signal(barrier, inc=1, device_id=(s + ds, r + dr), device_id_type=MESH)

    def edges(b, carry):
        for f in range(4):
            acc = zero
            for j in range(BX):
                at = 4 * (j + 2)
                moved = pltpu.roll(xm[b * BX + j, f], at, 1)
                acc = jnp.where((lane >= at - 2) & (lane < at + 2), moved, acc)
            edge[b, f] = acc
        return carry

    lax.fori_loop(0, nb, edges, 0)

    lower = jnp.broadcast_to(low[...], (8, lanes))
    upper = jnp.broadcast_to(upp[...], (8, lanes))
    first = jnp.concatenate([ginv[l * cols:l * cols + 1, :] for l in range(levels)], axis=0)
    final = jnp.concatenate([ginv[(l + 1) * cols - 1:(l + 1) * cols, :] for l in range(levels)], axis=0)
    coef[s, 0] = jnp.broadcast_to(first[:, 0:1], (8, lanes)) * lower
    coef[s, 1] = jnp.broadcast_to(final[:, 0:1], (8, lanes)) * lower
    coef[s, 2] = jnp.broadcast_to(first[:, cols - 1:cols], (8, lanes)) * upper
    coef[s, 3] = jnp.broadcast_to(final[:, cols - 1:cols], (8, lanes)) * upper

    def listed(dest, source):
        base = jnp.clip(dest, 0, n - 1) * nb
        count = jnp.int32(0)
        picks = [(jnp.int32(0), jnp.int32(0)) for _ in range(CAP)]
        for i in range(nb):
            g = base + i - offs[base + i]
            hit = (g >= source * nb) & (g < source * nb + nb)
            for k in range(CAP):
                here = hit & (count == k)
                picks[k] = (
                    jnp.where(here, jnp.int32(i), picks[k][0]),
                    jnp.where(here, g - source * nb, picks[k][1]),
                )
            count = count + jnp.where(hit, 1, 0)
        return picks

    for e, delta in enumerate(DELTA):
        outgoing = listed(s + delta, s)
        incoming = listed(s, s - delta)
        for k in range(CAP):
            blist[k * 4 + e] = outgoing[k][1]
            ilist[k * 4 + e] = incoming[k][0]
    own = listed(s, s)
    for k in range(CAP):
        blist[REMOTE + k] = own[k][1]
        ilist[REMOTE + k] = own[k][0]

    pl.semaphore_wait(
        barrier, n - 1 + sum(jnp.where(valid(ds, dr), 1, 0) for ds, dr in diagonal)
    )

    halo = [
        (1, 0, xm.at[pl.ds(cols - 2, 2)], side_rows.at[pl.ds(0, 2)]),
        (-1, 0, xm.at[pl.ds(0, 2)], side_rows.at[pl.ds(2, 2)]),
        (0, 1, edge, edge_lo.at[pl.ds(1, nb)]),
        (0, -1, edge, edge_hi.at[pl.ds(1, nb)]),
        (1, 1, edge.at[nb - 1], edge_lo.at[0]),
        (1, -1, edge.at[nb - 1], edge_hi.at[0]),
        (-1, 1, edge.at[0], edge_lo.at[nb + 1]),
        (-1, -1, edge.at[0], edge_hi.at[nb + 1]),
    ]

    def halo_copy(q):
        ds, dr, source, target = halo[q]
        return pltpu.make_async_remote_copy(
            src_ref=source, dst_ref=target, send_sem=halo_s.at[q], recv_sem=halo_r.at[q],
            device_id=(s + ds, r + dr), device_id_type=MESH,
        )

    for q in range(8):
        @pl.when(valid(halo[q][0], halo[q][1]))
        def _(q=q):
            halo_copy(q).start()

    def share(buffer, sends, recvs, d):
        return pltpu.make_async_remote_copy(
            src_ref=buffer.at[s], dst_ref=buffer.at[s], send_sem=sends.at[d],
            recv_sem=recvs.at[s], device_id=(d, r), device_id_type=MESH,
        )

    def shared(buffer, sends, recvs, d):
        return pltpu.make_async_remote_copy(
            src_ref=buffer.at[d], dst_ref=buffer.at[d], send_sem=sends.at[d],
            recv_sem=recvs.at[d], device_id=(d, r), device_id_type=MESH,
        )

    def others(act):
        def step(d, carry):
            @pl.when(d != s)
            def _():
                act(d)
            return carry
        lax.fori_loop(0, n, step, 0)

    def part_copy(slot, e, lo, size, sends, recvs, index):
        return pltpu.make_async_remote_copy(
            src_ref=send.at[slot, pl.ds(lo, size)], dst_ref=recv.at[slot, pl.ds(lo, size)],
            send_sem=sends.at[index], recv_sem=recvs.at[index],
            device_id=(s + DELTA[e], r), device_id_type=MESH,
        )

    def centre(into, slot, b):
        def row(j, carry):
            for f in range(4):
                into[slot, j, f] = xm[b * BX + j, f]
            return carry
        lax.fori_loop(0, BX, row, 0, unroll=4)

    def rim(into, slot, b):
        for j in range(5):
            for f in range(4):
                into[slot, BX + j, f] = rims[b, j, f]

    for e, delta in enumerate(DELTA):
        @pl.when(valid(delta, 0))
        def _(e=e):
            centre(send, e, blist[e])
            part_copy(e, e, 0, BX, slot_s, slot_r, e).start()

    others(lambda d: share(coef, coef_s, coef_r, d).start())

    for q in range(8):
        @pl.when(valid(-halo[q][0], -halo[q][1]))
        def _(q=q):
            halo_copy(q).wait_recv()

    before = ((lane + 2) & 3) < 2

    def make_rims(b, carry):
        for f in range(4):
            mid = jnp.where(before, edge_lo[b + 1, f], edge_hi[b + 1, f])
            prev = jnp.where(before, edge_lo[b, f], edge_hi[b, f])
            after = jnp.where(before, edge_lo[b + 2, f], edge_hi[b + 2, f])
            mid = jnp.where((lane >= 126) | (lane < 6), pltpu.roll(prev, 64, 1), mid)
            rims[b, 4, f] = jnp.where((lane >= 70) & (lane < 78), pltpu.roll(after, 64, 1), mid)
        return carry

    lax.fori_loop(0, nb, make_rims, 0)

    for b in range(nb):
        for f in range(4):
            for j in range(2):
                rims[b, j, f] = xm[b * BX - 2 + j, f] if b else side_rows[j, f]
                rims[b, 2 + j, f] = xm[b * BX + BX + j, f] if b < nb - 1 else side_rows[2 + j, f]

    for e, delta in enumerate(DELTA):
        @pl.when(valid(delta, 0))
        def _(e=e):
            rim(send, e, blist[e])
            part_copy(e, e, BX, 5, rim_s, rim_r, e).start()

    for k in range(1, CAP):
        for e, delta in enumerate(DELTA):
            @pl.when(valid(delta, 0))
            def _(e=e, slot=k * 4 + e):
                centre(send, slot, blist[slot])
                rim(send, slot, blist[slot])
                part_copy(slot, e, 0, ROWS, slot_s, slot_r, slot).start()

    for l in range(levels):
        def spike(x, carry, l=l):
            g = ginv[pl.ds(l * cols + x * 8, 8), :]
            spikes[0, l, pl.ds(x * 8, 8), :] = (
                jnp.broadcast_to(g[:, 0:1], (8, lanes)) * jnp.broadcast_to(low[l:l + 1, :], (8, lanes))
            )
            spikes[1, l, pl.ds(x * 8, 8), :] = (
                jnp.broadcast_to(g[:, cols - 1:cols], (8, lanes))
                * jnp.broadcast_to(upp[l:l + 1, :], (8, lanes))
            )
            return carry
        lax.fori_loop(0, cols // 8, spike, 0)

    def advect(buffer, slot):
        i = ilist[slot]

        def weigh(j, carry):
            for q, w in enumerate(weights_of(shx[i * BX + j])):
                wgt[j, q] = w
            for q, w in enumerate(weights_of(shy[i * BX + j])):
                wgt[j, 5 + q] = w
            return carry

        lax.fori_loop(0, BX, weigh, 0, unroll=2)

        def field(f, carry):
            side = buffer[slot, BX + 4, f]
            rows = []
            for x in range(BX + 4):
                at = BX + x if x < 2 else (x - 2 if x < BX + 2 else x)
                mid = buffer[slot, at, f]
                rimmed = side if x == 0 else pltpu.roll(side, lanes - 4 * x, 1)
                rows.append((
                    pltpu.roll(jnp.where(lane >= 126, rimmed, mid), 2, 1),
                    pltpu.roll(jnp.where(lane >= 127, rimmed, mid), 1, 1),
                    mid,
                    pltpu.roll(jnp.where(lane < 1, rimmed, mid), lanes - 1, 1),
                    pltpu.roll(jnp.where(lane < 2, rimmed, mid), lanes - 2, 1),
                ))
                if x >= 4:
                    j = x - 4
                    wy = [wgt[j, 5 + q] for q in range(5)]
                    total = None
                    for a in range(5):
                        part = wy[0] * rows[j + a][0]
                        for q in range(1, 5):
                            part = part + wy[q] * rows[j + a][q]
                        part = wgt[j, a] * part
                        total = part if total is None else total + part
                    adv[slot, pl.ds(f * levels * BX + j, levels, stride=BX), :] = total
            return carry

        lax.fori_loop(0, 4, field, 0)

    def local_slot(k, carry):
        slot = REMOTE + k
        b = blist[slot]
        centre(recv, slot, b)
        rim(recv, slot, b)
        advect(recv, slot)
        return carry

    lax.fori_loop(0, CAP, local_slot, 0)

    others(lambda d: shared(coef, coef_s, coef_r, d).wait_recv())

    def pivot_step(d, gain):
        ll, tl, lr, tr = (coef[d, q] for q in range(4))
        inverse = 1.0 / (1.0 - ll * gain)
        ratio = tl * gain * inverse
        work[d, 0] = gain
        work[d, 1] = inverse
        work[d, 2] = ratio
        return tr + ratio * lr

    lax.fori_loop(0, n, pivot_step, zero)

    def arrive(slot, lo, size, recvs):
        e = lax.rem(slot, jnp.int32(4))
        delta = (2 - lax.div(e, jnp.int32(2))) * (1 - 2 * lax.rem(e, jnp.int32(2)))

        @pl.when(valid(-delta, 0))
        def _():
            pltpu.make_async_remote_copy(
                src_ref=send.at[slot, pl.ds(lo, size)], dst_ref=recv.at[slot, pl.ds(lo, size)],
                send_sem=slot_s.at[slot], recv_sem=recvs.at[slot],
                device_id=(s + delta, r), device_id_type=MESH,
            ).wait_recv()

    def first_slot(slot, carry):
        arrive(slot, 0, BX, slot_r)
        arrive(slot, BX, 5, rim_r)
        advect(recv, slot)
        return carry

    def later_slot(slot, carry):
        arrive(slot, 0, ROWS, slot_r)
        advect(recv, slot)
        return carry

    lax.fori_loop(0, 4, first_slot, 0)
    lax.fori_loop(4, REMOTE, later_slot, 0)

    runs = []
    for i in range(nb):
        g = s * nb + i - offs[s * nb + i]
        runs.append(lax.shift_right_arithmetic(g, jnp.int32(nb.bit_length() - 1)))
    for i in range(nb):
        count = jnp.int32(0)
        for j in range(i):
            count = count + jnp.where(runs[j] == runs[i], 1, 0)
        count = jnp.minimum(count, CAP - 1)
        gap = s - runs[i]
        place = REMOTE + count
        for e, delta in enumerate(DELTA):
            place = jnp.where(gap == delta, count * 4 + e, place)

        def put(l, carry, i=i, place=place):
            for w in range(2):
                at = pl.multiple_of((w * levels + l) * BX, BX)
                solved[w, l, pl.ds(i * BX, BX), :] = adv[place, pl.ds(at, BX), :]
                at = pl.multiple_of(((w + 2) * levels + l) * BX, BX)
                tracers[w, l, pl.ds(i * BX, BX), :] = adv[place, pl.ds(at, BX), :]
            return carry

        lax.fori_loop(0, levels, put, 0)

    def solve(l, carry):
        right = jnp.concatenate([solved[0, l], solved[1, l]], axis=1)
        g = ginv[pl.ds(pl.multiple_of(l * cols, cols), cols), :]
        out = jnp.dot(g, right, precision=lax.Precision.HIGHEST, preferred_element_type=jnp.float32)
        for w in range(2):
            part = out[:, w * lanes:(w + 1) * lanes]
            solved[w, l] = part
            iface[s, w, pl.ds(l, 1), :] = part[0:1]
            iface[s, 2 + w, pl.ds(l, 1), :] = part[cols - 1:cols]
        return carry

    lax.fori_loop(0, levels, solve, 0)

    others(lambda d: share(iface, if_s, if_r, d).start())
    others(lambda d: shared(iface, if_s, if_r, d).wait_recv())

    def forward(d, behind):
        ll, tl, ratio = coef[d, 0], coef[d, 1], work[d, 2]
        after = []
        for w in range(2):
            lead = iface[d, w] - ll * behind[w]
            work[d, 3 + w] = lead
            work[d, 5 + w] = behind[w]
            after.append(iface[d, 2 + w] - tl * behind[w] + ratio * lead)
        return tuple(after)

    lax.fori_loop(0, n, forward, (zero, zero))

    def backward(k, ahead):
        d = n - 1 - k
        lr, inverse = coef[d, 2], work[d, 1]
        values = []
        for w in range(2):
            work[d, 7 + w] = ahead[w]
            values.append((work[d, 3 + w] - lr * ahead[w]) * inverse)
            work[d, 9 + w] = values[w]
        return tuple(values)

    lax.fori_loop(0, n - s, backward, (zero, zero))

    for w in range(2):
        left = work[s, 5 + w] - work[s, 0] * work[s, 9 + w]
        ahead = work[s, 7 + w]
        for l in range(levels):
            here = left[l:l + 1]
            there = ahead[l:l + 1]
            wind[w, l] = solved[w, l] - spikes[0, l] * here - spikes[1, l] * there

    for q in range(8):
        @pl.when(valid(halo[q][0], halo[q][1]))
        def _(q=q):
            halo_copy(q).wait_send()
    others(lambda d: share(coef, coef_s, coef_r, d).wait_send())
    others(lambda d: share(iface, if_s, if_r, d).wait_send())
    for e, delta in enumerate(DELTA):
        @pl.when(valid(delta, 0))
        def _(e=e):
            part_copy(e, e, 0, BX, slot_s, slot_r, e).wait_send()
            part_copy(e, e, BX, 5, rim_s, rim_r, e).wait_send()
            for k in range(1, CAP):
                part_copy(k * 4 + e, e, 0, ROWS, slot_s, slot_r, k * 4 + e).wait_send()


def local(n, m, fields, shift_x, shift_y, block_offset, group_inverse, lower, upper):
    nf, levels, cols, lanes = fields.shape
    nb = cols // BX
    vmem = pl.BlockSpec(memory_space=pltpu.VMEM)
    f32 = jnp.float32
    tile = (8, lanes)
    dma = pltpu.SemaphoreType.DMA
    return pl.pallas_call(
        functools.partial(kernel, n, m, nb),
        out_shape=(
            jax.ShapeDtypeStruct((2, levels, cols, lanes), f32),
            jax.ShapeDtypeStruct((2, levels, cols, lanes), f32),
        ),
        in_specs=[pl.BlockSpec(memory_space=pltpu.SMEM)] + [vmem] * 6,
        out_specs=(vmem, vmem),
        scratch_shapes=[
            pltpu.VMEM((4, nf) + tile, f32),
            pltpu.VMEM((nb, nf) + tile, f32),
            pltpu.VMEM((nb + 2, nf) + tile, f32),
            pltpu.VMEM((nb + 2, nf) + tile, f32),
            pltpu.VMEM((nb, 5, nf) + tile, f32),
            pltpu.VMEM((REMOTE, ROWS, nf) + tile, f32),
            pltpu.VMEM((SLOTS, ROWS, nf) + tile, f32),
            pltpu.VMEM((SLOTS, (nf * levels + 1) * BX, lanes), f32),
            pltpu.VMEM((BX, 10) + tile, f32),
            pltpu.VMEM((2, levels, cols, lanes), f32),
            pltpu.VMEM((2, levels, cols, lanes), f32),
            pltpu.VMEM((n, 4) + tile, f32),
            pltpu.VMEM((n, 4) + tile, f32),
            pltpu.VMEM((n, 11) + tile, f32),
            pltpu.SMEM((SLOTS,), jnp.int32),
            pltpu.SMEM((SLOTS,), jnp.int32),
            dma((8,)), dma((8,)), dma((REMOTE,)), dma((REMOTE,)), dma((4,)), dma((4,)),
            dma((n,)), dma((n,)), dma((n,)), dma((n,)),
        ],
        compiler_params=pltpu.CompilerParams(
            collective_id=0, has_side_effects=True, vmem_limit_bytes=50 * 1024 * 1024
        ),
    )(
        block_offset[:, 0],
        fields.transpose(2, 0, 1, 3),
        shift_x.transpose(1, 0, 2),
        shift_y.transpose(1, 0, 2),
        group_inverse.reshape(-1, cols),
        lower,
        upper,
    )


def solution(mesh):
    return jax.shard_map(
        functools.partial(local, mesh.shape["gx"], mesh.shape["gy"]),
        mesh=mesh,
        in_specs=(
            P(None, None, "gx", "gy"),
            P(None, "gx", "gy"),
            P(None, "gx", "gy"),
            P(None, "gy"),
            P(None, "gx", None),
            P(None, "gx"),
            P(None, "gx"),
        ),
        out_specs=(P(None, None, "gx", "gy"), P(None, None, "gx", "gy")),
        check_vma=False,
    )
```

```python
import functools

import jax
import jax.numpy as jnp
from jax import lax
from jax.experimental import pallas as pl
from jax.experimental.pallas import tpu as pltpu
from jax.sharding import PartitionSpec as P

BX = 16
CAP = 4
DELTA = (2, -2, 1, -1)
REMOTE = CAP * len(DELTA)
SLOTS = REMOTE + CAP
ROWS = BX + 5
MESH = pl.DeviceIdType.MESH


def weights_of(shift):
    p = -shift
    a, b, c, d = p + 2.0, p + 1.0, p - 1.0, p - 2.0
    ab, cd = a * b, c * d
    pcd, pab = p * cd, p * ab
    return (
        b * pcd * (1.0 / 24.0),
        a * pcd * (-1.0 / 6.0),
        ab * cd * 0.25,
        pab * d * (-1.0 / 6.0),
        pab * c * (1.0 / 24.0),
    )


def kernel(
    n, m, nb,
    offs, xm, shx, shy, ginv, low, upp,
    wind, tracers,
    side_rows, edge, edge_lo, edge_hi, rims, send, recv, adv, wgt, solved, spikes, coef, iface, work,
    ilist, blist,
    halo_s, halo_r, slot_s, slot_r, rim_s, rim_r, coef_s, coef_r, if_s, if_r,
):
    levels, cols, lanes = 8, nb * BX, 128
    s, r = lax.axis_index("gx"), lax.axis_index("gy")
    lane = lax.broadcasted_iota(jnp.int32, (8, lanes), 1)
    zero = jnp.zeros((8, lanes), jnp.float32)

    def valid(ds, dr):
        return (s + ds >= 0) & (s + ds < n) & (r + dr >= 0) & (r + dr < m)

    for f in range(4):
        for x in range(4):
            side_rows[x, f] = zero
        for b in range(nb + 2):
            edge_lo[b, f] = zero
            edge_hi[b, f] = zero

    barrier = pltpu.get_barrier_semaphore()
    diagonal = [(ds, dr) for ds in (-1, 0, 1) for dr in (-1, 1)]

    def greet(d, carry):
        @pl.when(d != s)
        def _():
            pl.semaphore_signal(barrier, inc=1, device_id=(d, r), device_id_type=MESH)
        return carry

    lax.fori_loop(0, n, greet, 0)
    for ds, dr in diagonal:
        @pl.when(valid(ds, dr))
        def _():
            pl.semaphore_signal(barrier, inc=1, device_id=(s + ds, r + dr), device_id_type=MESH)

    def edges(b, carry):
        for f in range(4):
            acc = zero
            for j in range(BX):
                at = 4 * (j + 2)
                moved = pltpu.roll(xm[b * BX + j, f], at, 1)
                acc = jnp.where((lane >= at - 2) & (lane < at + 2), moved, acc)
            edge[b, f] = acc
        return carry

    lax.fori_loop(0, nb, edges, 0)

    level = lax.broadcasted_iota(jnp.int32, (8, lanes), 0)
    lower, upper = zero, zero
    for l in range(levels):
        lower = jnp.where(level == l, low[l], lower)
        upper = jnp.where(level == l, upp[l], upper)
    first = jnp.concatenate([ginv[l * cols:l * cols + 1, :] for l in range(levels)], axis=0)
    final = jnp.concatenate([ginv[(l + 1) * cols - 1:(l + 1) * cols, :] for l in range(levels)], axis=0)
    coef[s, 0] = jnp.broadcast_to(first[:, 0:1], (8, lanes)) * lower
    coef[s, 1] = jnp.broadcast_to(final[:, 0:1], (8, lanes)) * lower
    coef[s, 2] = jnp.broadcast_to(first[:, cols - 1:cols], (8, lanes)) * upper
    coef[s, 3] = jnp.broadcast_to(final[:, cols - 1:cols], (8, lanes)) * upper

    def listed(dest, source):
        base = jnp.clip(dest, 0, n - 1) * nb
        count = jnp.int32(0)
        picks = [(jnp.int32(0), jnp.int32(0)) for _ in range(CAP)]
        for i in range(nb):
            g = base + i - offs[base + i]
            hit = (g >= source * nb) & (g < source * nb + nb)
            for k in range(CAP):
                here = hit & (count == k)
                picks[k] = (
                    jnp.where(here, jnp.int32(i), picks[k][0]),
                    jnp.where(here, g - source * nb, picks[k][1]),
                )
            count = count + jnp.where(hit, 1, 0)
        return picks

    for e, delta in enumerate(DELTA):
        outgoing = listed(s + delta, s)
        incoming = listed(s, s - delta)
        for k in range(CAP):
            blist[k * 4 + e] = outgoing[k][1]
            ilist[k * 4 + e] = incoming[k][0]
    own = listed(s, s)
    for k in range(CAP):
        blist[REMOTE + k] = own[k][1]
        ilist[REMOTE + k] = own[k][0]

    pl.semaphore_wait(
        barrier, n - 1 + sum(jnp.where(valid(ds, dr), 1, 0) for ds, dr in diagonal)
    )

    halo = [
        (1, 0, xm.at[pl.ds(cols - 2, 2)], side_rows.at[pl.ds(0, 2)]),
        (-1, 0, xm.at[pl.ds(0, 2)], side_rows.at[pl.ds(2, 2)]),
        (0, 1, edge, edge_lo.at[pl.ds(1, nb)]),
        (0, -1, edge, edge_hi.at[pl.ds(1, nb)]),
        (1, 1, edge.at[nb - 1], edge_lo.at[0]),
        (1, -1, edge.at[nb - 1], edge_hi.at[0]),
        (-1, 1, edge.at[0], edge_lo.at[nb + 1]),
        (-1, -1, edge.at[0], edge_hi.at[nb + 1]),
    ]

    def halo_copy(q):
        ds, dr, source, target = halo[q]
        return pltpu.make_async_remote_copy(
            src_ref=source, dst_ref=target, send_sem=halo_s.at[q], recv_sem=halo_r.at[q],
            device_id=(s + ds, r + dr), device_id_type=MESH,
        )

    for q in range(8):
        @pl.when(valid(halo[q][0], halo[q][1]))
        def _(q=q):
            halo_copy(q).start()

    def share(buffer, sends, recvs, d):
        return pltpu.make_async_remote_copy(
            src_ref=buffer.at[s], dst_ref=buffer.at[s], send_sem=sends.at[d],
            recv_sem=recvs.at[s], device_id=(d, r), device_id_type=MESH,
        )

    def shared(buffer, sends, recvs, d):
        return pltpu.make_async_remote_copy(
            src_ref=buffer.at[d], dst_ref=buffer.at[d], send_sem=sends.at[d],
            recv_sem=recvs.at[d], device_id=(d, r), device_id_type=MESH,
        )

    def others(act):
        def step(d, carry):
            @pl.when(d != s)
            def _():
                act(d)
            return carry
        lax.fori_loop(0, n, step, 0)

    def part_copy(slot, e, lo, size, sends, recvs, index):
        return pltpu.make_async_remote_copy(
            src_ref=send.at[slot, pl.ds(lo, size)], dst_ref=recv.at[slot, pl.ds(lo, size)],
            send_sem=sends.at[index], recv_sem=recvs.at[index],
            device_id=(s + DELTA[e], r), device_id_type=MESH,
        )

    def centre(into, slot, b):
        def row(j, carry):
            for f in range(4):
                into[slot, j, f] = xm[b * BX + j, f]
            return carry
        lax.fori_loop(0, BX, row, 0, unroll=4)

    def rim(into, slot, b):
        for j in range(5):
            for f in range(4):
                into[slot, BX + j, f] = rims[b, j, f]

    for e, delta in enumerate(DELTA):
        @pl.when(valid(delta, 0))
        def _(e=e):
            centre(send, e, blist[e])
            part_copy(e, e, 0, BX, slot_s, slot_r, e).start()

    others(lambda d: share(coef, coef_s, coef_r, d).start())

    for q in range(8):
        @pl.when(valid(-halo[q][0], -halo[q][1]))
        def _(q=q):
            halo_copy(q).wait_recv()

    before = ((lane + 2) & 3) < 2

    def make_rims(b, carry):
        for f in range(4):
            mid = jnp.where(before, edge_lo[b + 1, f], edge_hi[b + 1, f])
            prev = jnp.where(before, edge_lo[b, f], edge_hi[b, f])
            after = jnp.where(before, edge_lo[b + 2, f], edge_hi[b + 2, f])
            mid = jnp.where((lane >= 126) | (lane < 6), pltpu.roll(prev, 64, 1), mid)
            rims[b, 4, f] = jnp.where((lane >= 70) & (lane < 78), pltpu.roll(after, 64, 1), mid)
        return carry

    lax.fori_loop(0, nb, make_rims, 0)

    for b in range(nb):
        for f in range(4):
            for j in range(2):
                rims[b, j, f] = xm[b * BX - 2 + j, f] if b else side_rows[j, f]
                rims[b, 2 + j, f] = xm[b * BX + BX + j, f] if b < nb - 1 else side_rows[2 + j, f]

    for e, delta in enumerate(DELTA):
        @pl.when(valid(delta, 0))
        def _(e=e):
            rim(send, e, blist[e])
            part_copy(e, e, BX, 5, rim_s, rim_r, e).start()

    for k in range(1, CAP):
        for e, delta in enumerate(DELTA):
            @pl.when(valid(delta, 0))
            def _(e=e, slot=k * 4 + e):
                centre(send, slot, blist[slot])
                rim(send, slot, blist[slot])
                part_copy(slot, e, 0, ROWS, slot_s, slot_r, slot).start()

    for l in range(levels):
        def spike(x, carry, l=l):
            g = ginv[pl.ds(l * cols + x * 8, 8), :]
            spikes[0, l, pl.ds(x * 8, 8), :] = (
                jnp.broadcast_to(g[:, 0:1], (8, lanes)) * low[l]
            )
            spikes[1, l, pl.ds(x * 8, 8), :] = (
                jnp.broadcast_to(g[:, cols - 1:cols], (8, lanes)) * upp[l]
            )
            return carry
        lax.fori_loop(0, cols // 8, spike, 0)

    def advect(buffer, slot):
        i = ilist[slot]

        def weigh(j, carry):
            for q, w in enumerate(weights_of(shx[i * BX + j])):
                wgt[j, q] = w
            for q, w in enumerate(weights_of(shy[i * BX + j])):
                wgt[j, 5 + q] = w
            return carry

        lax.fori_loop(0, BX, weigh, 0, unroll=2)

        def field(f, carry):
            side = buffer[slot, BX + 4, f]
            rows = []
            for x in range(BX + 4):
                at = BX + x if x < 2 else (x - 2 if x < BX + 2 else x)
                mid = buffer[slot, at, f]
                rimmed = side if x == 0 else pltpu.roll(side, lanes - 4 * x, 1)
                rows.append((
                    pltpu.roll(jnp.where(lane >= 126, rimmed, mid), 2, 1),
                    pltpu.roll(jnp.where(lane >= 127, rimmed, mid), 1, 1),
                    mid,
                    pltpu.roll(jnp.where(lane < 1, rimmed, mid), lanes - 1, 1),
                    pltpu.roll(jnp.where(lane < 2, rimmed, mid), lanes - 2, 1),
                ))
                if x >= 4:
                    j = x - 4
                    wy = [wgt[j, 5 + q] for q in range(5)]
                    total = None
                    for a in range(5):
                        part = wy[0] * rows[j + a][0]
                        for q in range(1, 5):
                            part = part + wy[q] * rows[j + a][q]
                        part = wgt[j, a] * part
                        total = part if total is None else total + part
                    adv[slot, pl.ds(f * levels * BX + j, levels, stride=BX), :] = total
            return carry

        lax.fori_loop(0, 4, field, 0)

    def local_slot(k, carry):
        slot = REMOTE + k
        b = blist[slot]
        centre(recv, slot, b)
        rim(recv, slot, b)
        advect(recv, slot)
        return carry

    lax.fori_loop(0, CAP, local_slot, 0)

    others(lambda d: shared(coef, coef_s, coef_r, d).wait_recv())

    def pivot_step(d, gain):
        ll, tl, lr, tr = (coef[d, q] for q in range(4))
        inverse = 1.0 / (1.0 - ll * gain)
        ratio = tl * gain * inverse
        work[d, 0] = gain
        work[d, 1] = inverse
        work[d, 2] = ratio
        return tr + ratio * lr

    lax.fori_loop(0, n, pivot_step, zero)

    def arrive(slot, lo, size, recvs):
        e = lax.rem(slot, jnp.int32(4))
        delta = (2 - lax.div(e, jnp.int32(2))) * (1 - 2 * lax.rem(e, jnp.int32(2)))

        @pl.when(valid(-delta, 0))
        def _():
            pltpu.make_async_remote_copy(
                src_ref=send.at[slot, pl.ds(lo, size)], dst_ref=recv.at[slot, pl.ds(lo, size)],
                send_sem=slot_s.at[slot], recv_sem=recvs.at[slot],
                device_id=(s + delta, r), device_id_type=MESH,
            ).wait_recv()

    def first_slot(slot, carry):
        arrive(slot, 0, BX, slot_r)
        arrive(slot, BX, 5, rim_r)
        advect(recv, slot)
        return carry

    def later_slot(slot, carry):
        arrive(slot, 0, ROWS, slot_r)
        advect(recv, slot)
        return carry

    lax.fori_loop(0, 4, first_slot, 0)
    lax.fori_loop(4, REMOTE, later_slot, 0)

    runs = []
    for i in range(nb):
        g = s * nb + i - offs[s * nb + i]
        runs.append(lax.shift_right_arithmetic(g, jnp.int32(nb.bit_length() - 1)))
    for i in range(nb):
        count = jnp.int32(0)
        for j in range(i):
            count = count + jnp.where(runs[j] == runs[i], 1, 0)
        count = jnp.minimum(count, CAP - 1)
        gap = s - runs[i]
        place = REMOTE + count
        for e, delta in enumerate(DELTA):
            place = jnp.where(gap == delta, count * 4 + e, place)

        def put(l, carry, i=i, place=place):
            for w in range(2):
                at = pl.multiple_of((w * levels + l) * BX, BX)
                solved[w, l, pl.ds(i * BX, BX), :] = adv[place, pl.ds(at, BX), :]
                at = pl.multiple_of(((w + 2) * levels + l) * BX, BX)
                tracers[w, l, pl.ds(i * BX, BX), :] = adv[place, pl.ds(at, BX), :]
            return carry

        lax.fori_loop(0, levels, put, 0, unroll=4)

    def solve(l, carry):
        right = jnp.concatenate([solved[0, l], solved[1, l]], axis=1)
        g = ginv[pl.ds(pl.multiple_of(l * cols, cols), cols), :]
        out = jnp.dot(g, right, precision=lax.Precision.HIGHEST, preferred_element_type=jnp.float32)
        for w in range(2):
            part = out[:, w * lanes:(w + 1) * lanes]
            solved[w, l] = part
            iface[s, w, pl.ds(l, 1), :] = part[0:1]
            iface[s, 2 + w, pl.ds(l, 1), :] = part[cols - 1:cols]
        return carry

    lax.fori_loop(0, levels, solve, 0)

    others(lambda d: share(iface, if_s, if_r, d).start())
    others(lambda d: shared(iface, if_s, if_r, d).wait_recv())

    def forward(d, behind):
        ll, tl, ratio = coef[d, 0], coef[d, 1], work[d, 2]
        after = []
        for w in range(2):
            lead = iface[d, w] - ll * behind[w]
            work[d, 3 + w] = lead
            work[d, 5 + w] = behind[w]
            after.append(iface[d, 2 + w] - tl * behind[w] + ratio * lead)
        return tuple(after)

    lax.fori_loop(0, n, forward, (zero, zero))

    def backward(k, ahead):
        d = n - 1 - k
        lr, inverse = coef[d, 2], work[d, 1]
        values = []
        for w in range(2):
            work[d, 7 + w] = ahead[w]
            values.append((work[d, 3 + w] - lr * ahead[w]) * inverse)
            work[d, 9 + w] = values[w]
        return tuple(values)

    lax.fori_loop(0, n - s, backward, (zero, zero))

    for w in range(2):
        left = work[s, 5 + w] - work[s, 0] * work[s, 9 + w]
        ahead = work[s, 7 + w]
        for l in range(levels):
            here = left[l:l + 1]
            there = ahead[l:l + 1]
            wind[w, l] = solved[w, l] - spikes[0, l] * here - spikes[1, l] * there

    for q in range(8):
        @pl.when(valid(halo[q][0], halo[q][1]))
        def _(q=q):
            halo_copy(q).wait_send()
    others(lambda d: share(coef, coef_s, coef_r, d).wait_send())
    others(lambda d: share(iface, if_s, if_r, d).wait_send())
    for e, delta in enumerate(DELTA):
        @pl.when(valid(delta, 0))
        def _(e=e):
            part_copy(e, e, 0, BX, slot_s, slot_r, e).wait_send()
            part_copy(e, e, BX, 5, rim_s, rim_r, e).wait_send()
            for k in range(1, CAP):
                part_copy(k * 4 + e, e, 0, ROWS, slot_s, slot_r, k * 4 + e).wait_send()


def local(n, m, fields, shift_x, shift_y, block_offset, group_inverse, lower, upper):
    nf, levels, cols, lanes = fields.shape
    nb = cols // BX
    vmem = pl.BlockSpec(memory_space=pltpu.VMEM)
    smem = pl.BlockSpec(memory_space=pltpu.SMEM)
    f32 = jnp.float32
    tile = (8, lanes)
    dma = pltpu.SemaphoreType.DMA
    return pl.pallas_call(
        functools.partial(kernel, n, m, nb),
        out_shape=(
            jax.ShapeDtypeStruct((2, levels, cols, lanes), f32),
            jax.ShapeDtypeStruct((2, levels, cols, lanes), f32),
        ),
        in_specs=[smem] + [vmem] * 4 + [smem] * 2,
        out_specs=(vmem, vmem),
        scratch_shapes=[
            pltpu.VMEM((4, nf) + tile, f32),
            pltpu.VMEM((nb, nf) + tile, f32),
            pltpu.VMEM((nb + 2, nf) + tile, f32),
            pltpu.VMEM((nb + 2, nf) + tile, f32),
            pltpu.VMEM((nb, 5, nf) + tile, f32),
            pltpu.VMEM((REMOTE, ROWS, nf) + tile, f32),
            pltpu.VMEM((SLOTS, ROWS, nf) + tile, f32),
            pltpu.VMEM((SLOTS, (nf * levels + 1) * BX, lanes), f32),
            pltpu.VMEM((BX, 10) + tile, f32),
            pltpu.VMEM((2, levels, cols, lanes), f32),
            pltpu.VMEM((2, levels, cols, lanes), f32),
            pltpu.VMEM((n, 4) + tile, f32),
            pltpu.VMEM((n, 4) + tile, f32),
            pltpu.VMEM((n, 11) + tile, f32),
            pltpu.SMEM((SLOTS,), jnp.int32),
            pltpu.SMEM((SLOTS,), jnp.int32),
            dma((8,)), dma((8,)), dma((REMOTE,)), dma((REMOTE,)), dma((4,)), dma((4,)),
            dma((n,)), dma((n,)), dma((n,)), dma((n,)),
        ],
        compiler_params=pltpu.CompilerParams(
            collective_id=0, has_side_effects=True, vmem_limit_bytes=50 * 1024 * 1024
        ),
    )(
        block_offset[:, 0],
        fields.transpose(2, 0, 1, 3),
        shift_x.transpose(1, 0, 2),
        shift_y.transpose(1, 0, 2),
        group_inverse.reshape(-1, cols),
        lower[:, 0],
        upper[:, 0],
    )


def solution(mesh):
    return jax.shard_map(
        functools.partial(local, mesh.shape["gx"], mesh.shape["gy"]),
        mesh=mesh,
        in_specs=(
            P(None, None, "gx", "gy"),
            P(None, "gx", "gy"),
            P(None, "gx", "gy"),
            P(None, "gy"),
            P(None, "gx", None),
            P(None, "gx"),
            P(None, "gx"),
        ),
        out_specs=(P(None, None, "gx", "gy"), P(None, None, "gx", "gy")),
        check_vma=False,
    )
```
